32 devices in a mesh: rep: 2 (over x), dp: 8 (over z, y), tensor: 2 (over core).
Axes of the slice: x: 2, y: 2, z: 4, core: 2. Of those that a mesh axis runs over, the one named last changes fastest.
Arguments:
- tokens: bfloat16 [7168, 8192], P(('rep', 'dp'), 'tensor'), parts along dimension 0, may hold values from -6 to 6
- value_weight: bfloat16 [8192, 1024], P('tensor'), may hold values from -0.0625 to 0.0625
- pool_down: bfloat16 [8, 8192, 64], P('dp', 'tensor'), may hold values from -0.0625 to 0.0625
- pool_up: bfloat16 [8, 64, 1024], P('dp'), may hold values from -0.75 to 0.75
- block_adapter: int32 [1792, 1], P(('rep', 'dp')), parts along dimension 0, may hold values from 0 to 7; in each aligned block of 112 rows (0 to 111, 112 to 223, ...) at most 14 rows name the same one
- pool_slot: int32 [8], replicated, may hold values from 0 to 7, each once
Outputs:
- values: bfloat16 [7168, 1024], P(('rep', 'dp'), 'tensor'), parts along dimension 0
The draws below stay inside these ranges and needn't reach their ends.
There are 2 independent parts, one for each index of `rep`. The reference program is written for one: setup_inputs(seed, part) draws one part's arguments, and reference() takes and returns one part's arrays. A program takes and returns all parts, laid end to end along the dimension named above; an argument that names none is the same for every part. Nothing has to cross between parts.
Inputs may be any that keep to these rules, and one draw needn't show every extreme that they name: `block_adapter`: among the 112 blocks of one index of dp no adapter is named more than 14 times, a bound that some block reaches in them. `pool_slot`: A permutation of the pool rows.
All inputs are finite; a program needn't handle non-finite values.
Results may differ from the reference program's by a relative error of at most 0.001.
Values may be sent and summed in bfloat16 or wider, within the bound.
A program may use at most 64 MiB of HBM per device.

```python
import math
import jax
import jax.numpy as jnp
import numpy as np
from jax import lax

D = 8192
KV = 1024
R = 64
BLOCKS_DEV = 112
MOST = 14
ADAPTERS = 8
TOKENS = 3584
BLOCKS = 896


def levels(key, extent, shards, least, largest):
    factor_of, own = 1.0, jax.random.fold_in(key, 6)
    for axis_at, parts in shards:
        heights = jnp.exp(jax.random.uniform(jax.random.fold_in(own, axis_at), (parts,), jnp.float32, least / len(shards), largest / len(shards)))
        factor_of = factor_of * jnp.repeat(heights, extent[axis_at] // parts).reshape([-1 if axis == axis_at else 1 for axis in range(len(extent))])
    return factor_of


def deal_out(rng, own, number, rows, count, top, limit, lean):
    ranking = jax.random.permutation(rng, count)
    heavy_load, usual = shares(count, rows * top, limit, lean, True), shares(count, rows * top, limit, lean, False)
    places = jnp.arange(count)

    def named(sizes, offset_by):
        used = int((sizes > 0).sum())
        fixed = max(1, used // 4)
        shifted = fixed + (places - fixed + offset_by * (used - fixed)) % max(1, count - fixed)
        return jnp.zeros((count,), jnp.int32).at[ranking[jnp.where(places < fixed, places, shifted)]].set(jnp.asarray(sizes, jnp.int32))

    sizes = jnp.where(number % 4 == 0, named(heavy_load, number // 4), named(usual, number - number // 4 - 1))
    mixed = jax.random.permutation(jax.random.fold_in(own, 3), count)
    giver, sink = mixed[0:count // 2 * 2:2], mixed[1:count // 2 * 2:2]
    room = jnp.minimum(sizes[giver] - 1, limit - sizes[sink]) // 2
    room = jnp.where((giver == ranking[0]) | (sink == ranking[0]) | (sizes[sink] == 0), 0, jnp.maximum(room, 0))
    shifted = jax.random.randint(jax.random.fold_in(own, 4), (count // 2,), 0, 1 << 20) % (room + 1)
    sizes = sizes.at[giver].add(-shifted).at[sink].add(shifted)
    members = jnp.searchsorted(jnp.cumsum(sizes), jnp.arange(rows * top), side="right").astype(jnp.int32)
    table = members.reshape(top, rows).T
    table = table[jax.random.permutation(jax.random.fold_in(own, 1), rows)]
    offset_by = jax.random.randint(jax.random.fold_in(own, 2), (rows, 1), 0, top)
    return jnp.take_along_axis(table, (jnp.arange(top)[None, :] + offset_by) % top, axis=1)


def shares(amount, total, bound, lean, full):
    weights = [(1 << 20) // math.isqrt(grade ** lean) + 1 for grade in range(1, amount + 1)]
    largest = bound if full else min(bound, max(-(-total // amount), total * weights[0] // sum(weights)))
    least = 1 if total - largest >= amount - 1 else 0
    holding, rest = [largest] + [least] * (amount - 1), total - largest - least * (amount - 1)
    while rest > 0:
        movable = [i for i in range(1, amount) if holding[i] < largest] or [i for i in range(1, amount) if holding[i] < bound]
        whole, remaining = sum([weights[i] for i in movable]), rest
        for i in movable:
            extra = min(bound - holding[i], max(1, remaining * weights[i] // whole), rest)
            holding[i] = holding[i] + extra
            rest = rest - extra
    return np.array(holding)


def normal_values(own_key, extent, deviation, most, split=(), kind=jnp.bfloat16):
    drawn = jax.random.normal(own_key, extent, jnp.float32) * deviation
    if len(split) > 0:
        drawn = levels(own_key, extent, split, -0.22, 0.18) * drawn
    return jnp.clip(drawn, min=-most, max=most).astype(kind)


def setup_inputs(seed: int = 0, part: int = 0) -> dict:
    splits = jax.random.split(jax.random.key(seed), 7)
    part_splits = jax.random.split(jax.random.fold_in(splits[6], part), 7)
    tokens = normal_values(part_splits[0], (TOKENS, D), 1.0, 6.0, ((0, 8), (1, 2)))
    value_weight = normal_values(splits[1], (D, KV), D ** -0.5, 0.0625, ((0, 2),))
    pool_down = normal_values(splits[2], (ADAPTERS, D, R), D ** -0.5, 0.0625, ((0, 8), (1, 2)))
    pool_up = normal_values(splits[3], (ADAPTERS, R, KV), R ** -0.5, 0.75, ((0, 8),))
    block_adapter_keys = jax.random.split(jax.random.fold_in(part_splits[4], 1), BLOCKS // BLOCKS_DEV)
    block_adapter_turns = jax.random.permutation(jax.random.fold_in(part_splits[4], 3), BLOCKS // BLOCKS_DEV)
    block_adapter = jax.vmap(lambda own, number: deal_out(jax.random.fold_in(part_splits[4], 2), own, number, BLOCKS_DEV, ADAPTERS, 1, MOST, 2))(block_adapter_keys, block_adapter_turns).reshape((BLOCKS, 1))
    pool_slot = jax.random.permutation(splits[5], ADAPTERS).astype(jnp.int32)
    return {"tokens": tokens, "value_weight": value_weight, "pool_down": pool_down, "pool_up": pool_up, "block_adapter": block_adapter, "pool_slot": pool_slot}


def reference(tokens, value_weight, pool_down, pool_up, block_adapter, pool_slot):
    base = jnp.dot(tokens, value_weight, preferred_element_type=jnp.float32)
    nblocks = block_adapter.shape[0]
    width = tokens.shape[1]
    rows_in = tokens.shape[0] // nblocks
    pool_rows = jnp.take(pool_slot, block_adapter[:, 0].astype(jnp.int32), axis=0).astype(jnp.int32)
    blocked = tokens.reshape(nblocks, rows_in, width)

    def one_block(item):
        piece, row = item
        down = lax.dynamic_index_in_dim(pool_down, row, 0, keepdims=False)
        upper = lax.dynamic_index_in_dim(pool_up, row, 0, keepdims=False)
        shrink = jnp.dot(piece, down, preferred_element_type=jnp.float32)
        return jnp.dot(shrink, upper.astype(jnp.float32), precision=lax.Precision.HIGHEST)

    delta = lax.map(one_block, (blocked, pool_rows)).reshape(tokens.shape[0], value_weight.shape[1])
    return (base + delta).astype(jnp.bfloat16)
```

```python
import functools

import jax
import jax.numpy as jnp
from jax import lax
from jax.experimental import pallas as pl
from jax.experimental.pallas import tpu as pltpu
from jax.sharding import PartitionSpec as P

MESH = pl.DeviceIdType.MESH
LINE = 4


def moved_tokens(tokens, value_weight, pool_down, pool_up, block_adapter, pool_slot):
    peers = lax.axis_size("dp")
    cores = lax.axis_size("tensor")
    core = lax.axis_index("tensor")
    blocks = block_adapter.shape[0]
    width = tokens.shape[1]
    rows_in = tokens.shape[0] // blocks
    kv_full = value_weight.shape[1]
    kv_part = kv_full // cores
    most = max(2, (blocks + peers - 1) // peers)
    adapters = pool_slot.shape[0]
    ident = jnp.arange(adapters, dtype=jnp.int32)
    owner = jnp.sum(jnp.where(block_adapter == ident[None, :], pool_slot[None, :], 0), axis=1)
    same = owner[:, None] == owner[None, :]
    position = jnp.arange(blocks, dtype=jnp.int32)
    earlier = position[:, None] > position[None, :]
    rank_in = jnp.sum(jnp.where(same & earlier, 1, 0), axis=1)
    target = owner * most + rank_in
    flat_blocks = tokens.reshape(blocks, rows_in * width)
    outgoing = jnp.zeros((peers * most, rows_in * width), jnp.bfloat16).at[target].set(flat_blocks)
    outgoing = outgoing.reshape(peers, most * rows_in, width)
    base = jnp.dot(tokens, value_weight, preferred_element_type=jnp.float32)
    shrink_part = jnp.einsum(
        "pkd,dr->pkr",
        lax.all_to_all(outgoing, "dp", split_axis=0, concat_axis=0, tiled=True),
        pool_down[0],
        preferred_element_type=jnp.float32,
    )
    shrink_all = lax.psum(shrink_part, "tensor")
    columns = lax.dynamic_slice_in_dim(pool_up[0], core * kv_part, kv_part, 1).astype(jnp.float32)
    term = jnp.einsum("pkr,rc->pkc", shrink_all, columns, precision=lax.Precision.HIGHEST)
    answers = lax.all_to_all(term, "dp", split_axis=0, concat_axis=0, tiled=True)
    out_cols = answers.shape[2]
    answers = answers.reshape(peers * most, rows_in * out_cols)
    gathered = jnp.take(answers, target, axis=0).reshape(tokens.shape[0], out_cols)
    summed = lax.psum_scatter(base, "tensor", scatter_dimension=1, tiled=True)
    result = summed + gathered
    return result.astype(jnp.bfloat16)


def kernel(tok_hbm, w_hbm, down_hbm, up_hbm, adapter_ref, slot_ref, out_ref,
           tok, w, downs, ups, mine, other, base_in, acc, acc_in,
           local_sem, p_recv, c_recv, u_recv, x_recv, p_send, c_send, u_send, x_send,
           core_send, core_recv):
    x, dp, core = lax.axis_index("rep"), lax.axis_index("dp"), lax.axis_index("tensor")
    z, y = dp // 2, dp % 2
    rows, width = tok.shape
    rank = downs.shape[1]
    half = mine.shape[1]
    blocks = adapter_ref.shape[1]
    rows_in = rows // blocks
    adapters = slot_ref.shape[0]
    third = width * 3 // 8
    rest = width - 2 * third

    own_cols = pl.ds(pl.multiple_of(x * third, 128), third)
    far_cols = pl.ds(pl.multiple_of((1 - x) * third, 128), third)
    rest_cols = pl.ds(2 * third, rest)
    up_cols = pl.ds(pl.multiple_of(core * half, 128), half)
    other_cols = pl.ds(pl.multiple_of((1 - core) * half, 128), half)

    loads = [
        pltpu.make_async_copy(tok_hbm, tok, local_sem.at[0]),
        pltpu.make_async_copy(w_hbm.at[:, other_cols], w.at[1], local_sem.at[1]),
        pltpu.make_async_copy(w_hbm.at[:, up_cols], w.at[0], local_sem.at[2]),
        pltpu.make_async_copy(down_hbm, downs.at[dp], local_sem.at[3]),
        pltpu.make_async_copy(up_hbm.at[:, up_cols], ups.at[dp], local_sem.at[4]),
    ]

    has_up, has_low = z < LINE - 1, z > 0
    to_x, to_y, to_core = {"rep": 1 - x}, {"dp": z * 2 + 1 - y}, {"tensor": 1 - core}
    to_up = {"dp": jnp.minimum(dp + 2, 2 * LINE - 1)}
    to_low = {"dp": jnp.maximum(dp - 2, 0)}

    barrier = pltpu.get_barrier_semaphore()
    for near in (to_x, to_y, to_core):
        pl.semaphore_signal(barrier, inc=1, device_id=near, device_id_type=MESH)

    @pl.when(has_up)
    def _():
        pl.semaphore_signal(barrier, inc=1, device_id=to_up, device_id_type=MESH)

    @pl.when(has_low)
    def _():
        pl.semaphore_signal(barrier, inc=1, device_id=to_low, device_id_type=MESH)

    for load in loads:
        load.start()
    pl.semaphore_wait(barrier, 3 + jnp.where(has_up, 1, 0) + jnp.where(has_low, 1, 0))

    def p_copy(s, way, to, own=False):
        here = (down_hbm if own else downs.at[s]).at[:, own_cols]
        return pltpu.make_async_remote_copy(
            here, downs.at[s].at[:, own_cols], p_send.at[way, s], p_recv.at[s], to, MESH)

    def c_copy(s, way, to, own=False):
        here = (down_hbm if own else downs.at[s]).at[:, rest_cols]
        return pltpu.make_async_remote_copy(
            here, downs.at[s].at[:, rest_cols], c_send.at[way, s], c_recv.at[s], to, MESH)

    def u_copy(s, way, to, own=False):
        here = up_hbm.at[:, up_cols] if own else ups.at[s]
        return pltpu.make_async_remote_copy(
            here, ups.at[s], u_send.at[way, s], u_recv.at[s], to, MESH)

    def x_copy(s):
        return pltpu.make_async_remote_copy(
            downs.at[s].at[:, own_cols], downs.at[s].at[:, own_cols], x_send.at[s], x_recv.at[s], to_x, MESH)

    def x_wait(s):
        pltpu.make_async_remote_copy(
            downs.at[s].at[:, far_cols], downs.at[s].at[:, far_cols], x_send.at[s], x_recv.at[s], to_x, MESH).wait_recv()

    def zs(s, source_z, what):
        @pl.when(has_up & (source_z <= z))
        def _():
            what(0, to_up)

        @pl.when(has_low & (source_z >= z))
        def _():
            what(1, to_low)

    line = []
    for i in range(LINE - 1):
        rising = i + jnp.where(i >= z, 1, 0)
        falling = LINE - 1 - (i + jnp.where(i >= LINE - 1 - z, 1, 0))
        line.append(jnp.where(z < LINE // 2, rising, falling))

    def send_p(s, source_z, own=False):
        zs(s, source_z, lambda way, to: p_copy(s, way, to, own).start())
        p_copy(s, 2, to_y, own).start()

    def send_c(s, source_z, own=False):
        def both(way, to):
            c_copy(s, way, to, own).start()
            u_copy(s, way, to, own).start()
        zs(s, source_z, both)
        both(2, to_y)

    def got_p(s):
        p_copy(s, 2, to_y).wait_recv()

    def got_c(s):
        c_copy(s, 2, to_y).wait_recv()
        u_copy(s, 2, to_y).wait_recv()

    near = [v * 2 + y for v in line]
    beyond = [v * 2 + 1 - y for v in line]
    twin = z * 2 + 1 - y

    send_p(dp, z, True)
    send_c(dp, z, True)

    ids = jnp.broadcast_to(adapter_ref[...], (8, blocks))
    own_row = jnp.zeros((8, blocks), jnp.float32)
    for a in range(adapters):
        own_row = own_row + jnp.where(ids == a, slot_ref[a].astype(jnp.float32), 0.0)
    t_at = lax.broadcasted_iota(jnp.int32, (rows, blocks), 0)
    b_at = lax.broadcasted_iota(jnp.int32, (rows, blocks), 1) * rows_in
    spread = jnp.where((t_at >= b_at) & (t_at < b_at + rows_in), 1.0, 0.0).astype(jnp.bfloat16)
    owner = lax.dot_general(spread, own_row.astype(jnp.bfloat16), (((1,), (1,)), ((), ())),
                            preferred_element_type=jnp.float32)[:, :1]

    def dot_cols(s, cols):
        d = downs[s, :, cols]
        both = jnp.concatenate([d, d], axis=0)
        return lax.dot_general(tok[:, cols], both, (((1,), (1,)), ((), ())),
                               preferred_element_type=jnp.float32)

    def add(s, cols):
        acc[...] += jnp.where(owner == s.astype(jnp.float32), dot_cols(s, cols), 0.0)

    everything = pl.ds(0, width)
    step = width // 8

    def base(into, which):
        into[...] = jnp.dot(tok[:, :step], w[which, :step, :], preferred_element_type=jnp.float32)

        def body(k, _):
            at = pl.ds(pl.multiple_of(k * step, step), step)
            into[...] += jnp.dot(tok[:, at], w[which, at, :], preferred_element_type=jnp.float32)
            return 0
        lax.fori_loop(1, 8, body, 0)

    acc[...] = jnp.zeros_like(acc)
    for load in loads:
        load.wait()

    got_p(near[0])
    send_p(near[0], line[0])
    x_copy(near[0]).start()
    got_p(twin)
    x_copy(twin).start()
    base(other, 1)
    base_copy = pltpu.make_async_remote_copy(other, base_in, core_send.at[0], core_recv.at[0], to_core, MESH)
    base_copy.start()
    got_c(near[0])
    send_c(near[0], line[0])
    base(mine, 0)

    got_p(near[1])
    send_p(near[1], line[1])
    x_copy(near[1]).start()
    add(dp, everything)
    got_c(twin)
    got_p(beyond[0])
    x_copy(beyond[0]).start()
    got_c(near[1])
    send_c(near[1], line[1])
    x_wait(near[0])
    add(near[0], everything)

    got_p(near[2])
    send_p(near[2], line[2])
    x_copy(near[2]).start()
    got_p(beyond[1])
    x_copy(beyond[1]).start()
    got_c(near[2])
    send_c(near[2], line[2])
    x_wait(twin)
    add(twin, everything)
    x_wait(near[1])
    add(near[1], everything)
    got_p(beyond[2])
    x_copy(beyond[2]).start()

    got_c(beyond[0])
    x_wait(beyond[0])
    add(beyond[0], everything)
    x_wait(near[2])
    add(near[2], everything)
    got_c(beyond[1])
    x_wait(beyond[1])
    add(beyond[1], everything)
    add(beyond[2], own_cols)
    base_copy.wait()
    mine[...] += base_in[...]
    got_c(beyond[2])
    add(beyond[2], rest_cols)
    x_wait(beyond[2])
    add(beyond[2], far_cols)

    acc_copy = pltpu.make_async_remote_copy(acc, acc_in, core_send.at[1], core_recv.at[1], to_core, MESH)
    acc_copy.start()

    def sent(s, source_z, own=False):
        def each(way, to):
            p_copy(s, way, to, own).wait_send()
            c_copy(s, way, to, own).wait_send()
            u_copy(s, way, to, own).wait_send()
        zs(s, source_z, each)
        each(2, to_y)

    sent(dp, z, True)
    for s, v in zip(near, line):
        sent(s, v)
    for s in near + beyond + [twin]:
        x_copy(s).wait_send()

    acc_copy.wait()
    shrink = acc[...] + acc_in[...]
    peers = downs.shape[0]
    wide = jnp.concatenate([shrink] * (peers * rank // shrink.shape[1]), axis=1)
    at = lax.broadcasted_iota(jnp.int32, wide.shape, 1)
    which = (at // rank).astype(jnp.float32)
    wide = jnp.where(owner == which, wide, 0.0)
    high = wide.astype(jnp.bfloat16)
    low = (wide - high.astype(jnp.float32)).astype(jnp.bfloat16)
    upper = ups[...].reshape(peers * rank, half)
    delta = jnp.dot(high, upper, preferred_element_type=jnp.float32)
    delta += jnp.dot(low, upper, preferred_element_type=jnp.float32)
    out_ref[...] = (mine[...] + delta).astype(out_ref.dtype)


def moved_adapters(tokens, value_weight, pool_down, pool_up, block_adapter, pool_slot):
    peers = lax.axis_size("dp")
    rows, width = tokens.shape
    blocks = block_adapter.shape[0]
    rank = pool_down.shape[2]
    half = value_weight.shape[1] // lax.axis_size("tensor")
    down = jnp.swapaxes(pool_down[0], 0, 1)
    dma = pltpu.SemaphoreType.DMA
    hbm = pl.BlockSpec(memory_space=pl.ANY)
    flops = 2 * rows * width * 2 * half * 3
    return pl.pallas_call(
        kernel,
        out_shape=jax.ShapeDtypeStruct((rows, half), jnp.bfloat16),
        in_specs=[hbm, hbm, hbm, hbm, pl.BlockSpec(memory_space=pltpu.VMEM),
                  pl.BlockSpec(memory_space=pltpu.SMEM)],
        out_specs=pl.BlockSpec(memory_space=pltpu.VMEM),
        scratch_shapes=[
            pltpu.VMEM((rows, width), jnp.bfloat16),
            pltpu.VMEM((2, width, half), jnp.bfloat16),
            pltpu.VMEM((peers, rank, width), jnp.bfloat16),
            pltpu.VMEM((peers, rank, half), jnp.bfloat16),
            pltpu.VMEM((rows, half), jnp.float32),
            pltpu.VMEM((rows, half), jnp.float32),
            pltpu.VMEM((rows, half), jnp.float32),
            pltpu.VMEM((rows, 2 * rank), jnp.float32),
            pltpu.VMEM((rows, 2 * rank), jnp.float32),
            dma((5,)), dma((peers,)), dma((peers,)), dma((peers,)), dma((peers,)),
            dma((3, peers)), dma((3, peers)), dma((3, peers)), dma((peers,)),
            dma((2,)), dma((2,)),
        ],
        compiler_params=pltpu.CompilerParams(
            collective_id=0, has_side_effects=True, vmem_limit_bytes=44 * 2**20),
        cost_estimate=pl.CostEstimate(flops=flops, bytes_accessed=2 * (rows * width + width * 2 * half), transcendentals=0),
    )(tokens, value_weight, down, pool_up[0], block_adapter.reshape(1, blocks), pool_slot)


def solution(mesh):
    in_specs = (
        P(("rep", "dp"), "tensor"),
        P("tensor", None),
        P("dp", "tensor", None),
        P("dp", None, None),
        P(("rep", "dp"), None),
        P(),
    )
    out_specs = P(("rep", "dp"), "tensor")
    fits = mesh.shape["dp"] == 2 * LINE and mesh.shape["rep"] == 2 and mesh.shape["tensor"] == 2
    body = moved_adapters if fits else moved_tokens
    return jax.shard_map(body, mesh=mesh, in_specs=in_specs, out_specs=out_specs, check_vma=False)
```

```python
import functools

import jax
import jax.numpy as jnp
from jax import lax
from jax.experimental import pallas as pl
from jax.experimental.pallas import tpu as pltpu
from jax.sharding import PartitionSpec as P

MESH = pl.DeviceIdType.MESH
LINE = 4


def moved_tokens(tokens, value_weight, pool_down, pool_up, block_adapter, pool_slot):
    peers = lax.axis_size("dp")
    cores = lax.axis_size("tensor")
    core = lax.axis_index("tensor")
    blocks = block_adapter.shape[0]
    width = tokens.shape[1]
    rows_in = tokens.shape[0] // blocks
    kv_full = value_weight.shape[1]
    kv_part = kv_full // cores
    most = max(2, (blocks + peers - 1) // peers)
    adapters = pool_slot.shape[0]
    ident = jnp.arange(adapters, dtype=jnp.int32)
    owner = jnp.sum(jnp.where(block_adapter == ident[None, :], pool_slot[None, :], 0), axis=1)
    same = owner[:, None] == owner[None, :]
    position = jnp.arange(blocks, dtype=jnp.int32)
    earlier = position[:, None] > position[None, :]
    rank_in = jnp.sum(jnp.where(same & earlier, 1, 0), axis=1)
    target = owner * most + rank_in
    flat_blocks = tokens.reshape(blocks, rows_in * width)
    outgoing = jnp.zeros((peers * most, rows_in * width), jnp.bfloat16).at[target].set(flat_blocks)
    outgoing = outgoing.reshape(peers, most * rows_in, width)
    base = jnp.dot(tokens, value_weight, preferred_element_type=jnp.float32)
    shrink_part = jnp.einsum(
        "pkd,dr->pkr",
        lax.all_to_all(outgoing, "dp", split_axis=0, concat_axis=0, tiled=True),
        pool_down[0],
        preferred_element_type=jnp.float32,
    )
    shrink_all = lax.psum(shrink_part, "tensor")
    columns = lax.dynamic_slice_in_dim(pool_up[0], core * kv_part, kv_part, 1).astype(jnp.float32)
    term = jnp.einsum("pkr,rc->pkc", shrink_all, columns, precision=lax.Precision.HIGHEST)
    answers = lax.all_to_all(term, "dp", split_axis=0, concat_axis=0, tiled=True)
    out_cols = answers.shape[2]
    answers = answers.reshape(peers * most, rows_in * out_cols)
    gathered = jnp.take(answers, target, axis=0).reshape(tokens.shape[0], out_cols)
    summed = lax.psum_scatter(base, "tensor", scatter_dimension=1, tiled=True)
    result = summed + gathered
    return result.astype(jnp.bfloat16)


def kernel(tok_hbm, w_hbm, down_hbm, up_hbm, adapter_hbm, slot_hbm, out_ref,
           adapter_ref, slot_ref, tok, w, downs, ups, mine, other, base_in, acc, acc_in, last, last_in,
           local_sem, p_recv, c_recv, u_recv, x_recv, p_send, c_send, u_send, x_send,
           core_send, core_recv):
    x, dp, core = lax.axis_index("rep"), lax.axis_index("dp"), lax.axis_index("tensor")
    z, y = dp // 2, dp % 2
    rows, width = tok.shape
    rank = downs.shape[1]
    half = mine.shape[1]
    blocks = adapter_ref.shape[1]
    rows_in = rows // blocks
    adapters = slot_ref.shape[0]
    third = width * 3 // 8
    rest = width - 2 * third

    own_cols = pl.ds(pl.multiple_of(x * third, 128), third)
    far_cols = pl.ds(pl.multiple_of((1 - x) * third, 128), third)
    rest_cols = pl.ds(2 * third, rest)
    up_cols = pl.ds(pl.multiple_of(core * half, 128), half)
    other_cols = pl.ds(pl.multiple_of((1 - core) * half, 128), half)

    loads = [
        pltpu.make_async_copy(tok_hbm, tok, local_sem.at[0]),
        pltpu.make_async_copy(w_hbm.at[:, other_cols], w.at[1], local_sem.at[1]),
        pltpu.make_async_copy(w_hbm.at[:, up_cols], w.at[0], local_sem.at[2]),
        pltpu.make_async_copy(down_hbm, downs.at[dp], local_sem.at[3]),
        pltpu.make_async_copy(up_hbm.at[:, up_cols], ups.at[dp], local_sem.at[4]),
        pltpu.make_async_copy(adapter_hbm, adapter_ref, local_sem.at[5]),
        pltpu.make_async_copy(slot_hbm, slot_ref, local_sem.at[6]),
    ]

    has_up, has_low = z < LINE - 1, z > 0
    to_x, to_y, to_core = {"rep": 1 - x}, {"dp": z * 2 + 1 - y}, {"tensor": 1 - core}
    to_up = {"dp": jnp.minimum(dp + 2, 2 * LINE - 1)}
    to_low = {"dp": jnp.maximum(dp - 2, 0)}

    for load in loads:
        load.start()
    barrier = pltpu.get_barrier_semaphore()
    for near in (to_x, to_y, to_core):
        pl.semaphore_signal(barrier, inc=1, device_id=near, device_id_type=MESH)

    @pl.when(has_up)
    def _():
        pl.semaphore_signal(barrier, inc=1, device_id=to_up, device_id_type=MESH)

    @pl.when(has_low)
    def _():
        pl.semaphore_signal(barrier, inc=1, device_id=to_low, device_id_type=MESH)

    pl.semaphore_wait(barrier, 3 + jnp.where(has_up, 1, 0) + jnp.where(has_low, 1, 0))

    def p_copy(s, way, to, own=False):
        here = (down_hbm if own else downs.at[s]).at[:, own_cols]
        return pltpu.make_async_remote_copy(
            here, downs.at[s].at[:, own_cols], p_send.at[way, s], p_recv.at[s], to, MESH)

    def c_copy(s, way, to, own=False):
        here = (down_hbm if own else downs.at[s]).at[:, rest_cols]
        return pltpu.make_async_remote_copy(
            here, downs.at[s].at[:, rest_cols], c_send.at[way, s], c_recv.at[s], to, MESH)

    def u_copy(s, way, to, own=False):
        here = up_hbm.at[:, up_cols] if own else ups.at[s]
        return pltpu.make_async_remote_copy(
            here, ups.at[s], u_send.at[way, s], u_recv.at[s], to, MESH)

    def x_copy(s):
        return pltpu.make_async_remote_copy(
            downs.at[s].at[:, own_cols], downs.at[s].at[:, own_cols], x_send.at[s], x_recv.at[s], to_x, MESH)

    def x_wait(s):
        pltpu.make_async_remote_copy(
            downs.at[s].at[:, far_cols], downs.at[s].at[:, far_cols], x_send.at[s], x_recv.at[s], to_x, MESH).wait_recv()

    def zs(s, source_z, what):
        @pl.when(has_up & (source_z <= z))
        def _():
            what(0, to_up)

        @pl.when(has_low & (source_z >= z))
        def _():
            what(1, to_low)

    line = []
    for i in range(LINE - 1):
        rising = i + jnp.where(i >= z, 1, 0)
        falling = LINE - 1 - (i + jnp.where(i >= LINE - 1 - z, 1, 0))
        line.append(jnp.where(z < LINE // 2, rising, falling))

    def send_p(s, source_z, own=False):
        zs(s, source_z, lambda way, to: p_copy(s, way, to, own).start())
        p_copy(s, 2, to_y, own).start()

    def send_c(s, source_z, own=False):
        def both(way, to):
            u_copy(s, way, to, own).start()
            c_copy(s, way, to, own).start()
        zs(s, source_z, both)
        both(2, to_y)

    def got_p(s):
        p_copy(s, 2, to_y).wait_recv()

    def got_c(s):
        u_copy(s, 2, to_y).wait_recv()
        c_copy(s, 2, to_y).wait_recv()

    near = [v * 2 + y for v in line]
    beyond = [v * 2 + 1 - y for v in line]
    twin = z * 2 + 1 - y

    send_p(dp, z, True)
    send_c(dp, z, True)
    for load in loads[5:]:
        load.wait()

    ids = jnp.broadcast_to(adapter_ref[...], (8, blocks))
    own_row = jnp.zeros((8, blocks), jnp.float32)
    for a in range(adapters):
        own_row = own_row + jnp.where(ids == a, slot_ref[a].astype(jnp.float32), 0.0)
    t_at = lax.broadcasted_iota(jnp.int32, (rows, blocks), 0)
    b_at = lax.broadcasted_iota(jnp.int32, (rows, blocks), 1) * rows_in
    spread = jnp.where((t_at >= b_at) & (t_at < b_at + rows_in), 1.0, 0.0).astype(jnp.bfloat16)
    owner = lax.dot_general(spread, own_row.astype(jnp.bfloat16), (((1,), (1,)), ((), ())),
                            preferred_element_type=jnp.float32)[:, :1]

    def dot_cols(s, cols):
        d = downs[s, :, cols]
        both = jnp.concatenate([d, d], axis=0)
        return lax.dot_general(tok[:, cols], both, (((1,), (1,)), ((), ())),
                               preferred_element_type=jnp.float32)

    def add(s, cols, into=acc):
        into[...] += jnp.where(owner == s.astype(jnp.float32), dot_cols(s, cols), 0.0)

    def exchange(src, dst, at):
        return pltpu.make_async_remote_copy(src, dst, core_send.at[at], core_recv.at[at], to_core, MESH)

    everything = pl.ds(0, width)
    step = width // 8

    def base(into, which):
        into[...] = jnp.dot(tok[:, :step], w[which, :step, :], preferred_element_type=jnp.float32)

        def body(k, _):
            at = pl.ds(pl.multiple_of(k * step, step), step)
            into[...] += jnp.dot(tok[:, at], w[which, at, :], preferred_element_type=jnp.float32)
            return 0
        lax.fori_loop(1, 8, body, 0)

    acc[...] = jnp.zeros_like(acc)
    for load in loads[:5]:
        load.wait()

    def take_p(i):
        got_p(near[i])
        send_p(near[i], line[i])
        x_copy(near[i]).start()

    def take_c(i):
        got_c(near[i])
        send_c(near[i], line[i])

    take_p(0)
    got_p(twin)
    x_copy(twin).start()

    @pl.when(has_up & has_low)
    def _():
        take_p(1)

    base(other, 1)
    base_copy = exchange(other, base_in, 0)
    base_copy.start()
    take_c(0)

    @pl.when(has_up & has_low)
    def _():
        take_c(1)

    base(mine, 0)

    @pl.when(jnp.logical_not(has_up & has_low))
    def _():
        take_p(1)

    got_p(beyond[0])
    x_copy(beyond[0]).start()
    add(dp, everything)
    got_c(twin)

    @pl.when(jnp.logical_not(has_up & has_low))
    def _():
        take_c(1)

    x_wait(near[0])
    add(near[0], everything)

    take_p(2)
    got_p(beyond[1])
    x_copy(beyond[1]).start()
    x_wait(twin)
    add(twin, everything)
    take_c(2)
    x_wait(near[1])
    add(near[1], everything)
    got_p(beyond[2])
    x_copy(beyond[2]).start()

    got_c(beyond[0])
    x_wait(beyond[0])
    add(beyond[0], everything)
    x_wait(near[2])
    add(near[2], everything)
    got_c(beyond[1])
    x_wait(beyond[1])
    add(beyond[1], everything)
    acc_copy = exchange(acc, acc_in, 1)
    acc_copy.start()
    last[...] = jnp.zeros_like(last)
    add(beyond[2], own_cols, last)
    base_copy.wait()
    mine[...] += base_in[...]
    u_copy(beyond[2], 2, to_y).wait_recv()
    acc_copy.wait()

    def halves(value):
        high = value.astype(jnp.bfloat16)
        return high, (value - high.astype(jnp.float32)).astype(jnp.bfloat16)

    shrink = acc[...] + acc_in[...]
    peers = downs.shape[0]
    wide = jnp.concatenate([shrink] * (peers * rank // shrink.shape[1]), axis=1)
    which = (lax.broadcasted_iota(jnp.int32, wide.shape, 1) // rank).astype(jnp.float32)
    high, low = halves(jnp.where(owner == which, wide, 0.0))
    upper = ups[...].reshape(peers * rank, half)
    mine[...] += jnp.dot(high, upper, preferred_element_type=jnp.float32)
    mine[...] += jnp.dot(low, upper, preferred_element_type=jnp.float32)

    c_copy(beyond[2], 2, to_y).wait_recv()
    add(beyond[2], rest_cols, last)
    x_wait(beyond[2])
    add(beyond[2], far_cols, last)
    last_copy = exchange(last, last_in, 2)
    last_copy.start()

    def sent(s, source_z, own=False):
        def each(way, to):
            p_copy(s, way, to, own).wait_send()
            c_copy(s, way, to, own).wait_send()
            u_copy(s, way, to, own).wait_send()
        zs(s, source_z, each)
        each(2, to_y)

    sent(dp, z, True)
    for s, v in zip(near, line):
        sent(s, v)
    for s in near + beyond + [twin]:
        x_copy(s).wait_send()

    last_copy.wait()
    high, low = halves(last[...] + last_in[...])
    row = ups[beyond[2]]
    left = lax.broadcasted_iota(jnp.int32, high.shape, 1) < rank
    both = jnp.where(left, high.astype(jnp.float32), low.astype(jnp.float32)).astype(jnp.bfloat16)
    delta = jnp.dot(both, jnp.concatenate([row, row], axis=0), preferred_element_type=jnp.float32)
    out_ref[...] = (mine[...] + delta).astype(out_ref.dtype)


def moved_adapters(tokens, value_weight, pool_down, pool_up, block_adapter, pool_slot):
    peers = lax.axis_size("dp")
    rows, width = tokens.shape
    blocks = block_adapter.shape[0]
    rank = pool_down.shape[2]
    half = value_weight.shape[1] // lax.axis_size("tensor")
    down = jnp.swapaxes(pool_down[0], 0, 1)
    dma = pltpu.SemaphoreType.DMA
    hbm = pl.BlockSpec(memory_space=pltpu.HBM)
    flops = 2 * rows * width * 2 * half * 3
    return pl.pallas_call(
        kernel,
        out_shape=jax.ShapeDtypeStruct((rows, half), jnp.bfloat16),
        in_specs=[hbm] * 6,
        out_specs=pl.BlockSpec(memory_space=pltpu.VMEM),
        scratch_shapes=[
            pltpu.VMEM((1, blocks), jnp.int32),
            pltpu.SMEM(pool_slot.shape, jnp.int32),
            pltpu.VMEM((rows, width), jnp.bfloat16),
            pltpu.VMEM((2, width, half), jnp.bfloat16),
            pltpu.VMEM((peers, rank, width), jnp.bfloat16),
            pltpu.VMEM((peers, rank, half), jnp.bfloat16),
            pltpu.VMEM((rows, half), jnp.float32),
            pltpu.VMEM((rows, half), jnp.float32),
            pltpu.VMEM((rows, half), jnp.float32),
            pltpu.VMEM((rows, 2 * rank), jnp.float32),
            pltpu.VMEM((rows, 2 * rank), jnp.float32),
            pltpu.VMEM((rows, 2 * rank), jnp.float32),
            pltpu.VMEM((rows, 2 * rank), jnp.float32),
            dma((7,)), dma((peers,)), dma((peers,)), dma((peers,)), dma((peers,)),
            dma((3, peers)), dma((3, peers)), dma((3, peers)), dma((peers,)),
            dma((3,)), dma((3,)),
        ],
        compiler_params=pltpu.CompilerParams(
            collective_id=0, has_side_effects=True, vmem_limit_bytes=64 * 2**20 - 2**16),
        cost_estimate=pl.CostEstimate(flops=flops, bytes_accessed=2 * (rows * width + width * 2 * half), transcendentals=0),
    )(tokens, value_weight, down, pool_up[0], block_adapter.reshape(1, blocks), pool_slot)


def solution(mesh):
    in_specs = (
        P(("rep", "dp"), "tensor"),
        P("tensor", None),
        P("dp", "tensor", None),
        P("dp", None, None),
        P(("rep", "dp"), None),
        P(),
    )
    out_specs = P(("rep", "dp"), "tensor")
    fits = mesh.shape["dp"] == 2 * LINE and mesh.shape["rep"] == 2 and mesh.shape["tensor"] == 2
    body = moved_adapters if fits else moved_tokens
    return jax.shard_map(body, mesh=mesh, in_specs=in_specs, out_specs=out_specs, check_vma=False)
```

```python
import functools

import jax
import jax.numpy as jnp
from jax import lax
from jax.experimental import pallas as pl
from jax.experimental.pallas import tpu as pltpu
from jax.sharding import PartitionSpec as P

MESH = pl.DeviceIdType.MESH
LINE = 4


def moved_tokens(tokens, value_weight, pool_down, pool_up, block_adapter, pool_slot):
    peers = lax.axis_size("dp")
    cores = lax.axis_size("tensor")
    core = lax.axis_index("tensor")
    blocks = block_adapter.shape[0]
    width = tokens.shape[1]
    rows_in = tokens.shape[0] // blocks
    kv_full = value_weight.shape[1]
    kv_part = kv_full // cores
    most = max(2, (blocks + peers - 1) // peers)
    adapters = pool_slot.shape[0]
    ident = jnp.arange(adapters, dtype=jnp.int32)
    owner = jnp.sum(jnp.where(block_adapter == ident[None, :], pool_slot[None, :], 0), axis=1)
    same = owner[:, None] == owner[None, :]
    position = jnp.arange(blocks, dtype=jnp.int32)
    earlier = position[:, None] > position[None, :]
    rank_in = jnp.sum(jnp.where(same & earlier, 1, 0), axis=1)
    target = owner * most + rank_in
    flat_blocks = tokens.reshape(blocks, rows_in * width)
    outgoing = jnp.zeros((peers * most, rows_in * width), jnp.bfloat16).at[target].set(flat_blocks)
    outgoing = outgoing.reshape(peers, most * rows_in, width)
    base = jnp.dot(tokens, value_weight, preferred_element_type=jnp.float32)
    shrink_part = jnp.einsum(
        "pkd,dr->pkr",
        lax.all_to_all(outgoing, "dp", split_axis=0, concat_axis=0, tiled=True),
        pool_down[0],
        preferred_element_type=jnp.float32,
    )
    shrink_all = lax.psum(shrink_part, "tensor")
    columns = lax.dynamic_slice_in_dim(pool_up[0], core * kv_part, kv_part, 1).astype(jnp.float32)
    term = jnp.einsum("pkr,rc->pkc", shrink_all, columns, precision=lax.Precision.HIGHEST)
    answers = lax.all_to_all(term, "dp", split_axis=0, concat_axis=0, tiled=True)
    out_cols = answers.shape[2]
    answers = answers.reshape(peers * most, rows_in * out_cols)
    gathered = jnp.take(answers, target, axis=0).reshape(tokens.shape[0], out_cols)
    summed = lax.psum_scatter(base, "tensor", scatter_dimension=1, tiled=True)
    result = summed + gathered
    return result.astype(jnp.bfloat16)


def kernel(tok_hbm, w_hbm, down_hbm, up_hbm, adapter_hbm, slot_hbm, out_ref,
           adapter_ref, slot_ref, tok, w, downs, ups, mine, other, base_in, acc, acc_in, last, last_in,
           local_sem, p_recv, c_recv, u_recv, x_recv, p_send, c_send, u_send, x_send,
           core_send, core_recv):
    x, dp, core = lax.axis_index("rep"), lax.axis_index("dp"), lax.axis_index("tensor")
    z, y = dp // 2, dp % 2
    rows, width = tok.shape
    rank = downs.shape[1]
    half = mine.shape[1]
    blocks = adapter_ref.shape[1]
    rows_in = rows // blocks
    adapters = slot_ref.shape[0]
    third = width * 3 // 8
    rest = width - 2 * third

    own_cols = pl.ds(pl.multiple_of(x * third, 128), third)
    far_cols = pl.ds(pl.multiple_of((1 - x) * third, 128), third)
    rest_cols = pl.ds(2 * third, rest)
    up_cols = pl.ds(pl.multiple_of(core * half, 128), half)
    other_cols = pl.ds(pl.multiple_of((1 - core) * half, 128), half)

    loads = [
        pltpu.make_async_copy(tok_hbm, tok, local_sem.at[0]),
        pltpu.make_async_copy(w_hbm.at[:, other_cols], w.at[1], local_sem.at[1]),
        pltpu.make_async_copy(w_hbm.at[:, up_cols], w.at[0], local_sem.at[2]),
        pltpu.make_async_copy(down_hbm, downs.at[dp], local_sem.at[3]),
        pltpu.make_async_copy(up_hbm.at[:, up_cols], ups.at[dp], local_sem.at[4]),
        pltpu.make_async_copy(adapter_hbm, adapter_ref, local_sem.at[5]),
        pltpu.make_async_copy(slot_hbm, slot_ref, local_sem.at[6]),
    ]

    has_up, has_low = z < LINE - 1, z > 0
    to_x, to_y, to_core = {"rep": 1 - x}, {"dp": z * 2 + 1 - y}, {"tensor": 1 - core}
    to_up = {"dp": jnp.minimum(dp + 2, 2 * LINE - 1)}
    to_low = {"dp": jnp.maximum(dp - 2, 0)}

    for load in loads:
        load.start()
    barrier = pltpu.get_barrier_semaphore()
    for near in (to_x, to_y, to_core):
        pl.semaphore_signal(barrier, inc=1, device_id=near, device_id_type=MESH)

    @pl.when(has_up)
    def _():
        pl.semaphore_signal(barrier, inc=1, device_id=to_up, device_id_type=MESH)

    @pl.when(has_low)
    def _():
        pl.semaphore_signal(barrier, inc=1, device_id=to_low, device_id_type=MESH)

    pl.semaphore_wait(barrier, 3 + jnp.where(has_up, 1, 0) + jnp.where(has_low, 1, 0))

    def p_copy(s, way, to, own=False):
        here = (down_hbm if own else downs.at[s]).at[:, own_cols]
        return pltpu.make_async_remote_copy(
            here, downs.at[s].at[:, own_cols], p_send.at[way, s], p_recv.at[s], to, MESH)

    def c_copy(s, way, to, own=False):
        here = (down_hbm if own else downs.at[s]).at[:, rest_cols]
        return pltpu.make_async_remote_copy(
            here, downs.at[s].at[:, rest_cols], c_send.at[way, s], c_recv.at[s], to, MESH)

    def u_copy(s, way, to, own=False):
        here = up_hbm.at[:, up_cols] if own else ups.at[s]
        return pltpu.make_async_remote_copy(
            here, ups.at[s], u_send.at[way, s], u_recv.at[s], to, MESH)

    def x_copy(s):
        return pltpu.make_async_remote_copy(
            downs.at[s].at[:, own_cols], downs.at[s].at[:, own_cols], x_send.at[s], x_recv.at[s], to_x, MESH)

    def x_wait(s):
        pltpu.make_async_remote_copy(
            downs.at[s].at[:, far_cols], downs.at[s].at[:, far_cols], x_send.at[s], x_recv.at[s], to_x, MESH).wait_recv()

    def zs(s, source_z, what):
        @pl.when(has_up & (source_z <= z))
        def _():
            what(0, to_up)

        @pl.when(has_low & (source_z >= z))
        def _():
            what(1, to_low)

    line = []
    for i in range(LINE - 1):
        rising = i + jnp.where(i >= z, 1, 0)
        falling = LINE - 1 - (i + jnp.where(i >= LINE - 1 - z, 1, 0))
        line.append(jnp.where(z < LINE // 2, rising, falling))

    def send_p(s, source_z, own=False):
        p_copy(s, 2, to_y, own).start()
        zs(s, source_z, lambda way, to: p_copy(s, way, to, own).start())

    def send_c(s, source_z, own=False):
        def both(way, to):
            u_copy(s, way, to, own).start()
            c_copy(s, way, to, own).start()
        both(2, to_y)
        zs(s, source_z, both)

    def got_p(s):
        p_copy(s, 2, to_y).wait_recv()

    def got_c(s):
        u_copy(s, 2, to_y).wait_recv()
        c_copy(s, 2, to_y).wait_recv()

    near = [v * 2 + y for v in line]
    beyond = [v * 2 + 1 - y for v in line]
    twin = z * 2 + 1 - y

    send_p(dp, z, True)
    send_c(dp, z, True)
    for load in loads[5:]:
        load.wait()

    ids = jnp.broadcast_to(adapter_ref[...], (8, blocks))
    own_row = jnp.zeros((8, blocks), jnp.float32)
    for a in range(adapters):
        own_row = own_row + jnp.where(ids == a, slot_ref[a].astype(jnp.float32), 0.0)
    t_at = lax.broadcasted_iota(jnp.int32, (rows, blocks), 0)
    b_at = lax.broadcasted_iota(jnp.int32, (rows, blocks), 1) * rows_in
    spread = jnp.where((t_at >= b_at) & (t_at < b_at + rows_in), 1.0, 0.0).astype(jnp.bfloat16)
    owner = lax.dot_general(spread, own_row.astype(jnp.bfloat16), (((1,), (1,)), ((), ())),
                            preferred_element_type=jnp.float32)[:, :1]

    def dot_cols(s, cols):
        d = downs[s, :, cols]
        both = jnp.concatenate([d, d], axis=0)
        return lax.dot_general(tok[:, cols], both, (((1,), (1,)), ((), ())),
                               preferred_element_type=jnp.float32)

    def add(s, cols, into=acc):
        into[...] += jnp.where(owner == s.astype(jnp.float32), dot_cols(s, cols), 0.0)

    def exchange(src, dst, at):
        return pltpu.make_async_remote_copy(src, dst, core_send.at[at], core_recv.at[at], to_core, MESH)

    everything = pl.ds(0, width)
    step = width // 8

    def base(into, which):
        into[...] = jnp.dot(tok[:, :step], w[which, :step, :], preferred_element_type=jnp.float32)

        def body(k, _):
            at = pl.ds(pl.multiple_of(k * step, step), step)
            into[...] += jnp.dot(tok[:, at], w[which, at, :], preferred_element_type=jnp.float32)
            return 0
        lax.fori_loop(1, 8, body, 0)

    acc[...] = jnp.zeros_like(acc)
    for load in loads[:5]:
        load.wait()

    def take_p(i):
        got_p(near[i])
        x_copy(near[i]).start()
        send_p(near[i], line[i])

    def take_c(i):
        got_c(near[i])
        send_c(near[i], line[i])

    take_p(0)
    got_p(twin)
    x_copy(twin).start()

    @pl.when(has_up & has_low)
    def _():
        take_p(1)

    base(other, 1)
    base_copy = exchange(other, base_in, 0)
    base_copy.start()
    take_c(0)

    @pl.when(has_up & has_low)
    def _():
        take_c(1)

    @pl.when(jnp.logical_not(has_up & has_low))
    def _():
        take_p(1)

    got_p(beyond[0])
    x_copy(beyond[0]).start()
    add(dp, everything)
    got_c(twin)

    @pl.when(jnp.logical_not(has_up & has_low))
    def _():
        take_c(1)

    x_wait(near[0])
    add(near[0], everything)

    take_p(2)
    got_p(beyond[1])
    x_copy(beyond[1]).start()
    base(mine, 0)
    x_wait(twin)
    add(twin, everything)
    take_c(2)
    x_wait(near[1])
    add(near[1], everything)
    got_p(beyond[2])
    x_copy(beyond[2]).start()

    got_c(beyond[0])
    x_wait(beyond[0])
    add(beyond[0], everything)
    x_wait(near[2])
    add(near[2], everything)
    got_c(beyond[1])
    x_wait(beyond[1])
    add(beyond[1], everything)
    acc_copy = exchange(acc, acc_in, 1)
    acc_copy.start()
    last[...] = jnp.zeros_like(last)
    add(beyond[2], own_cols, last)
    base_copy.wait()
    mine[...] += base_in[...]
    u_copy(beyond[2], 2, to_y).wait_recv()
    acc_copy.wait()

    def halves(value):
        high = value.astype(jnp.bfloat16)
        return high, (value - high.astype(jnp.float32)).astype(jnp.bfloat16)

    shrink = acc[...] + acc_in[...]
    peers = downs.shape[0]
    wide = jnp.concatenate([shrink] * (peers * rank // shrink.shape[1]), axis=1)
    which = (lax.broadcasted_iota(jnp.int32, wide.shape, 1) // rank).astype(jnp.float32)
    high, low = halves(jnp.where(owner == which, wide, 0.0))
    upper = ups[...].reshape(peers * rank, half)
    mine[...] += jnp.dot(high, upper, preferred_element_type=jnp.float32)
    mine[...] += jnp.dot(low, upper, preferred_element_type=jnp.float32)

    c_copy(beyond[2], 2, to_y).wait_recv()
    add(beyond[2], rest_cols, last)
    x_wait(beyond[2])
    add(beyond[2], far_cols, last)
    last_copy = exchange(last, last_in, 2)
    last_copy.start()

    def sent(s, source_z, own=False):
        def each(way, to):
            p_copy(s, way, to, own).wait_send()
            c_copy(s, way, to, own).wait_send()
            u_copy(s, way, to, own).wait_send()
        zs(s, source_z, each)
        each(2, to_y)

    sent(dp, z, True)
    for s, v in zip(near, line):
        sent(s, v)
    for s in near + beyond + [twin]:
        x_copy(s).wait_send()

    last_copy.wait()
    high, low = halves(last[...] + last_in[...])
    row = ups[beyond[2]]
    left = lax.broadcasted_iota(jnp.int32, high.shape, 1) < rank
    both = jnp.where(left, high.astype(jnp.float32), low.astype(jnp.float32)).astype(jnp.bfloat16)
    delta = jnp.dot(both, jnp.concatenate([row, row], axis=0), preferred_element_type=jnp.float32)
    out_ref[...] = (mine[...] + delta).astype(out_ref.dtype)


def moved_adapters(tokens, value_weight, pool_down, pool_up, block_adapter, pool_slot):
    peers = lax.axis_size("dp")
    rows, width = tokens.shape
    blocks = block_adapter.shape[0]
    rank = pool_down.shape[2]
    half = value_weight.shape[1] // lax.axis_size("tensor")
    down = jnp.swapaxes(pool_down[0], 0, 1)
    dma = pltpu.SemaphoreType.DMA
    hbm = pl.BlockSpec(memory_space=pltpu.HBM)
    flops = 2 * rows * width * 2 * half * 3
    return pl.pallas_call(
        kernel,
        out_shape=jax.ShapeDtypeStruct((rows, half), jnp.bfloat16),
        in_specs=[hbm] * 6,
        out_specs=pl.BlockSpec(memory_space=pltpu.VMEM),
        scratch_shapes=[
            pltpu.VMEM((1, blocks), jnp.int32),
            pltpu.SMEM(pool_slot.shape, jnp.int32),
            pltpu.VMEM((rows, width), jnp.bfloat16),
            pltpu.VMEM((2, width, half), jnp.bfloat16),
            pltpu.VMEM((peers, rank, width), jnp.bfloat16),
            pltpu.VMEM((peers, rank, half), jnp.bfloat16),
            pltpu.VMEM((rows, half), jnp.float32),
            pltpu.VMEM((rows, half), jnp.float32),
            pltpu.VMEM((rows, half), jnp.float32),
            pltpu.VMEM((rows, 2 * rank), jnp.float32),
            pltpu.VMEM((rows, 2 * rank), jnp.float32),
            pltpu.VMEM((rows, 2 * rank), jnp.float32),
            pltpu.VMEM((rows, 2 * rank), jnp.float32),
            dma((7,)), dma((peers,)), dma((peers,)), dma((peers,)), dma((peers,)),
            dma((3, peers)), dma((3, peers)), dma((3, peers)), dma((peers,)),
            dma((3,)), dma((3,)),
        ],
        compiler_params=pltpu.CompilerParams(
            collective_id=0, has_side_effects=True, vmem_limit_bytes=64 * 2**20 - 2**16),
        cost_estimate=pl.CostEstimate(flops=flops, bytes_accessed=2 * (rows * width + width * 2 * half), transcendentals=0),
    )(tokens, value_weight, down, pool_up[0], block_adapter.reshape(1, blocks), pool_slot)


def solution(mesh):
    in_specs = (
        P(("rep", "dp"), "tensor"),
        P("tensor", None),
        P("dp", "tensor", None),
        P("dp", None, None),
        P(("rep", "dp"), None),
        P(),
    )
    out_specs = P(("rep", "dp"), "tensor")
    fits = mesh.shape["dp"] == 2 * LINE and mesh.shape["rep"] == 2 and mesh.shape["tensor"] == 2
    body = moved_adapters if fits else moved_tokens
    return jax.shard_map(body, mesh=mesh, in_specs=in_specs, out_specs=out_specs, check_vma=False)
```

```python
import functools

import jax
import jax.numpy as jnp
from jax import lax
from jax.experimental import pallas as pl
from jax.experimental.pallas import tpu as pltpu
from jax.sharding import PartitionSpec as P

MESH = pl.DeviceIdType.MESH
LINE = 4


def moved_tokens(tokens, value_weight, pool_down, pool_up, block_adapter, pool_slot):
    peers = lax.axis_size("dp")
    cores = lax.axis_size("tensor")
    core = lax.axis_index("tensor")
    blocks = block_adapter.shape[0]
    width = tokens.shape[1]
    rows_in = tokens.shape[0] // blocks
    kv_full = value_weight.shape[1]
    kv_part = kv_full // cores
    most = max(2, (blocks + peers - 1) // peers)
    adapters = pool_slot.shape[0]
    ident = jnp.arange(adapters, dtype=jnp.int32)
    owner = jnp.sum(jnp.where(block_adapter == ident[None, :], pool_slot[None, :], 0), axis=1)
    same = owner[:, None] == owner[None, :]
    position = jnp.arange(blocks, dtype=jnp.int32)
    earlier = position[:, None] > position[None, :]
    rank_in = jnp.sum(jnp.where(same & earlier, 1, 0), axis=1)
    target = owner * most + rank_in
    flat_blocks = tokens.reshape(blocks, rows_in * width)
    outgoing = jnp.zeros((peers * most, rows_in * width), jnp.bfloat16).at[target].set(flat_blocks)
    outgoing = outgoing.reshape(peers, most * rows_in, width)
    base = jnp.dot(tokens, value_weight, preferred_element_type=jnp.float32)
    shrink_part = jnp.einsum(
        "pkd,dr->pkr",
        lax.all_to_all(outgoing, "dp", split_axis=0, concat_axis=0, tiled=True),
        pool_down[0],
        preferred_element_type=jnp.float32,
    )
    shrink_all = lax.psum(shrink_part, "tensor")
    columns = lax.dynamic_slice_in_dim(pool_up[0], core * kv_part, kv_part, 1).astype(jnp.float32)
    term = jnp.einsum("pkr,rc->pkc", shrink_all, columns, precision=lax.Precision.HIGHEST)
    answers = lax.all_to_all(term, "dp", split_axis=0, concat_axis=0, tiled=True)
    out_cols = answers.shape[2]
    answers = answers.reshape(peers * most, rows_in * out_cols)
    gathered = jnp.take(answers, target, axis=0).reshape(tokens.shape[0], out_cols)
    summed = lax.psum_scatter(base, "tensor", scatter_dimension=1, tiled=True)
    result = summed + gathered
    return result.astype(jnp.bfloat16)


def kernel(tok_hbm, w_hbm, down_hbm, up_hbm, adapter_hbm, slot_hbm, out_ref,
           adapter_ref, slot_ref, tok, w, downs, ups, mine, other, base_in, acc, acc_in, last, last_in,
           local_sem, p_recv, c_recv, u_recv, x_recv, p_send, c_send, u_send, x_send,
           core_send, core_recv):
    x, dp, core = lax.axis_index("rep"), lax.axis_index("dp"), lax.axis_index("tensor")
    z, y = dp // 2, dp % 2
    rows, width = tok.shape
    rank = downs.shape[1]
    half = mine.shape[1]
    blocks = adapter_ref.shape[1]
    rows_in = rows // blocks
    adapters = slot_ref.shape[0]
    third = width * 3 // 8
    rest = width - 2 * third

    own_cols = pl.ds(pl.multiple_of(x * third, 128), third)
    far_cols = pl.ds(pl.multiple_of((1 - x) * third, 128), third)
    rest_cols = pl.ds(2 * third, rest)
    up_cols = pl.ds(pl.multiple_of(core * half, 128), half)
    other_cols = pl.ds(pl.multiple_of((1 - core) * half, 128), half)

    loads = [
        pltpu.make_async_copy(tok_hbm, tok, local_sem.at[0]),
        pltpu.make_async_copy(w_hbm.at[:, other_cols], w.at[1], local_sem.at[1]),
        pltpu.make_async_copy(w_hbm.at[:, up_cols], w.at[0], local_sem.at[2]),
        pltpu.make_async_copy(down_hbm, downs.at[dp], local_sem.at[3]),
        pltpu.make_async_copy(up_hbm.at[:, up_cols], ups.at[dp], local_sem.at[4]),
        pltpu.make_async_copy(adapter_hbm, adapter_ref, local_sem.at[5]),
        pltpu.make_async_copy(slot_hbm, slot_ref, local_sem.at[6]),
    ]

    has_up, has_low = z < LINE - 1, z > 0
    to_x, to_y, to_core = {"rep": 1 - x}, {"dp": z * 2 + 1 - y}, {"tensor": 1 - core}
    to_up = {"dp": jnp.minimum(dp + 2, 2 * LINE - 1)}
    to_low = {"dp": jnp.maximum(dp - 2, 0)}

    for load in loads[3:]:
        load.start()
    barrier = pltpu.get_barrier_semaphore()
    for near in (to_x, to_y, to_core):
        pl.semaphore_signal(barrier, inc=1, device_id=near, device_id_type=MESH)

    @pl.when(has_up)
    def _():
        pl.semaphore_signal(barrier, inc=1, device_id=to_up, device_id_type=MESH)

    @pl.when(has_low)
    def _():
        pl.semaphore_signal(barrier, inc=1, device_id=to_low, device_id_type=MESH)

    pl.semaphore_wait(barrier, 3 + jnp.where(has_up, 1, 0) + jnp.where(has_low, 1, 0))

    def p_copy(s, way, to, own=False):
        here = (down_hbm if own else downs.at[s]).at[:, own_cols]
        return pltpu.make_async_remote_copy(
            here, downs.at[s].at[:, own_cols], p_send.at[way, s], p_recv.at[s], to, MESH)

    def c_copy(s, way, to, own=False):
        here = (down_hbm if own else downs.at[s]).at[:, rest_cols]
        return pltpu.make_async_remote_copy(
            here, downs.at[s].at[:, rest_cols], c_send.at[way, s], c_recv.at[s], to, MESH)

    def u_copy(s, way, to, own=False):
        here = up_hbm.at[:, up_cols] if own else ups.at[s]
        return pltpu.make_async_remote_copy(
            here, ups.at[s], u_send.at[way, s], u_recv.at[s], to, MESH)

    def x_copy(s):
        return pltpu.make_async_remote_copy(
            downs.at[s].at[:, own_cols], downs.at[s].at[:, own_cols], x_send.at[s], x_recv.at[s], to_x, MESH)

    def x_wait(s):
        pltpu.make_async_remote_copy(
            downs.at[s].at[:, far_cols], downs.at[s].at[:, far_cols], x_send.at[s], x_recv.at[s], to_x, MESH).wait_recv()

    def zs(s, source_z, what):
        @pl.when(has_up & (source_z <= z))
        def _():
            what(0, to_up)

        @pl.when(has_low & (source_z >= z))
        def _():
            what(1, to_low)

    line = []
    for i in range(LINE - 1):
        rising = i + jnp.where(i >= z, 1, 0)
        falling = LINE - 1 - (i + jnp.where(i >= LINE - 1 - z, 1, 0))
        line.append(jnp.where(z < LINE // 2, rising, falling))

    def send_p(s, source_z, own=False):
        p_copy(s, 2, to_y, own).start()
        zs(s, source_z, lambda way, to: p_copy(s, way, to, own).start())

    def send_c(s, source_z, own=False):
        def both(way, to):
            u_copy(s, way, to, own).start()
            c_copy(s, way, to, own).start()
        both(2, to_y)
        zs(s, source_z, both)

    def got_p(s):
        p_copy(s, 2, to_y).wait_recv()

    def got_c(s):
        u_copy(s, 2, to_y).wait_recv()
        c_copy(s, 2, to_y).wait_recv()

    near = [v * 2 + y for v in line]
    beyond = [v * 2 + 1 - y for v in line]
    twin = z * 2 + 1 - y

    send_p(dp, z, True)
    send_c(dp, z, True)
    for load in loads[:3]:
        load.start()
    for load in loads[5:]:
        load.wait()

    ids = jnp.broadcast_to(adapter_ref[...], (8, blocks))
    own_row = jnp.zeros((8, blocks), jnp.float32)
    for a in range(adapters):
        own_row = own_row + jnp.where(ids == a, slot_ref[a].astype(jnp.float32), 0.0)
    t_at = lax.broadcasted_iota(jnp.int32, (rows, blocks), 0)
    b_at = lax.broadcasted_iota(jnp.int32, (rows, blocks), 1) * rows_in
    spread = jnp.where((t_at >= b_at) & (t_at < b_at + rows_in), 1.0, 0.0).astype(jnp.bfloat16)
    owner = lax.dot_general(spread, own_row.astype(jnp.bfloat16), (((1,), (1,)), ((), ())),
                            preferred_element_type=jnp.float32)[:, :1]

    def dot_cols(s, cols):
        d = downs[s, :, cols]
        both = jnp.concatenate([d, d], axis=0)
        return lax.dot_general(tok[:, cols], both, (((1,), (1,)), ((), ())),
                               preferred_element_type=jnp.float32)

    def add(s, cols, into=acc):
        into[...] += jnp.where(owner == s.astype(jnp.float32), dot_cols(s, cols), 0.0)

    def exchange(src, dst, at):
        return pltpu.make_async_remote_copy(src, dst, core_send.at[at], core_recv.at[at], to_core, MESH)

    everything = pl.ds(0, width)
    step = width // 8

    def base(into, which):
        into[...] = jnp.dot(tok[:, :step], w[which, :step, :], preferred_element_type=jnp.float32)

        def body(k, _):
            at = pl.ds(pl.multiple_of(k * step, step), step)
            into[...] += jnp.dot(tok[:, at], w[which, at, :], preferred_element_type=jnp.float32)
            return 0
        lax.fori_loop(1, 8, body, 0)

    acc[...] = jnp.zeros_like(acc)
    for load in loads[:5]:
        load.wait()

    def take_p(i):
        got_p(near[i])
        x_copy(near[i]).start()
        send_p(near[i], line[i])

    def take_c(i):
        got_c(near[i])
        send_c(near[i], line[i])

    take_p(0)
    got_p(twin)
    x_copy(twin).start()

    @pl.when(has_up & has_low)
    def _():
        take_p(1)

    base(other, 1)
    base_copy = exchange(other, base_in, 0)
    base_copy.start()
    take_c(0)

    @pl.when(has_up & has_low)
    def _():
        take_c(1)

    @pl.when(jnp.logical_not(has_up & has_low))
    def _():
        take_p(1)

    got_p(beyond[0])
    x_copy(beyond[0]).start()
    add(dp, everything)
    got_c(twin)

    @pl.when(jnp.logical_not(has_up & has_low))
    def _():
        take_c(1)

    x_wait(near[0])
    add(near[0], everything)

    take_p(2)
    got_p(beyond[1])
    x_copy(beyond[1]).start()
    base(mine, 0)
    x_wait(twin)
    add(twin, everything)
    take_c(2)
    x_wait(near[1])
    add(near[1], everything)
    got_p(beyond[2])
    x_copy(beyond[2]).start()

    got_c(beyond[0])
    x_wait(beyond[0])
    add(beyond[0], everything)
    x_wait(near[2])
    add(near[2], everything)
    got_c(beyond[1])
    x_wait(beyond[1])
    add(beyond[1], everything)
    acc_copy = exchange(acc, acc_in, 1)
    acc_copy.start()
    last[...] = jnp.zeros_like(last)
    add(beyond[2], own_cols, last)
    base_copy.wait()
    mine[...] += base_in[...]
    u_copy(beyond[2], 2, to_y).wait_recv()
    acc_copy.wait()

    def halves(value):
        high = value.astype(jnp.bfloat16)
        return high, (value - high.astype(jnp.float32)).astype(jnp.bfloat16)

    shrink = acc[...] + acc_in[...]
    peers = downs.shape[0]
    wide = jnp.concatenate([shrink] * (peers * rank // shrink.shape[1]), axis=1)
    which = (lax.broadcasted_iota(jnp.int32, wide.shape, 1) // rank).astype(jnp.float32)
    high, low = halves(jnp.where(owner == which, wide, 0.0))
    upper = ups[...].reshape(peers * rank, half)
    mine[...] += jnp.dot(high, upper, preferred_element_type=jnp.float32)
    mine[...] += jnp.dot(low, upper, preferred_element_type=jnp.float32)

    c_copy(beyond[2], 2, to_y).wait_recv()
    add(beyond[2], rest_cols, last)
    x_wait(beyond[2])
    add(beyond[2], far_cols, last)
    last_copy = exchange(last, last_in, 2)
    last_copy.start()

    def sent(s, source_z, own=False):
        def each(way, to):
            p_copy(s, way, to, own).wait_send()
            c_copy(s, way, to, own).wait_send()
            u_copy(s, way, to, own).wait_send()
        zs(s, source_z, each)
        each(2, to_y)

    sent(dp, z, True)
    for s, v in zip(near, line):
        sent(s, v)
    for s in near + beyond + [twin]:
        x_copy(s).wait_send()

    last_copy.wait()
    high, low = halves(last[...] + last_in[...])
    row = ups[beyond[2]]
    left = lax.broadcasted_iota(jnp.int32, high.shape, 1) < rank
    both = jnp.where(left, high.astype(jnp.float32), low.astype(jnp.float32)).astype(jnp.bfloat16)
    delta = jnp.dot(both, jnp.concatenate([row, row], axis=0), preferred_element_type=jnp.float32)
    out_ref[...] = (mine[...] + delta).astype(out_ref.dtype)


def moved_adapters(tokens, value_weight, pool_down, pool_up, block_adapter, pool_slot):
    peers = lax.axis_size("dp")
    rows, width = tokens.shape
    blocks = block_adapter.shape[0]
    rank = pool_down.shape[2]
    half = value_weight.shape[1] // lax.axis_size("tensor")
    down = jnp.swapaxes(pool_down[0], 0, 1)
    dma = pltpu.SemaphoreType.DMA
    hbm = pl.BlockSpec(memory_space=pltpu.HBM)
    flops = 2 * rows * width * 2 * half * 3
    return pl.pallas_call(
        kernel,
        out_shape=jax.ShapeDtypeStruct((rows, half), jnp.bfloat16),
        in_specs=[hbm] * 6,
        out_specs=pl.BlockSpec(memory_space=pltpu.VMEM),
        scratch_shapes=[
            pltpu.VMEM((1, blocks), jnp.int32),
            pltpu.SMEM(pool_slot.shape, jnp.int32),
            pltpu.VMEM((rows, width), jnp.bfloat16),
            pltpu.VMEM((2, width, half), jnp.bfloat16),
            pltpu.VMEM((peers, rank, width), jnp.bfloat16),
            pltpu.VMEM((peers, rank, half), jnp.bfloat16),
            pltpu.VMEM((rows, half), jnp.float32),
            pltpu.VMEM((rows, half), jnp.float32),
            pltpu.VMEM((rows, half), jnp.float32),
            pltpu.VMEM((rows, 2 * rank), jnp.float32),
            pltpu.VMEM((rows, 2 * rank), jnp.float32),
            pltpu.VMEM((rows, 2 * rank), jnp.float32),
            pltpu.VMEM((rows, 2 * rank), jnp.float32),
            dma((7,)), dma((peers,)), dma((peers,)), dma((peers,)), dma((peers,)),
            dma((3, peers)), dma((3, peers)), dma((3, peers)), dma((peers,)),
            dma((3,)), dma((3,)),
        ],
        compiler_params=pltpu.CompilerParams(
            collective_id=0, has_side_effects=True, vmem_limit_bytes=64 * 2**20 - 2**16),
        cost_estimate=pl.CostEstimate(flops=flops, bytes_accessed=2 * (rows * width + width * 2 * half), transcendentals=0),
    )(tokens, value_weight, down, pool_up[0], block_adapter.reshape(1, blocks), pool_slot)


def solution(mesh):
    in_specs = (
        P(("rep", "dp"), "tensor"),
        P("tensor", None),
        P("dp", "tensor", None),
        P("dp", None, None),
        P(("rep", "dp"), None),
        P(),
    )
    out_specs = P(("rep", "dp"), "tensor")
    fits = mesh.shape["dp"] == 2 * LINE and mesh.shape["rep"] == 2 and mesh.shape["tensor"] == 2
    body = moved_adapters if fits else moved_tokens
    return jax.shard_map(body, mesh=mesh, in_specs=in_specs, out_specs=out_specs, check_vma=False)
```
